32 devices in a mesh: feat: 2 (over x), samp: 16 (over z, y, core).
Axes of the slice: x: 2, y: 2, z: 4, core: 2. Of those that a mesh axis runs over, the one named last changes fastest.
Arguments:
- samples: bfloat16 [6144, 32768], P('samp', 'feat'), may hold values from -6 to 6
- factor: float32 [32768, 128], P(('feat', 'samp')), as said below
Outputs:
- factor_out: float32 [32768, 128], P(('feat', 'samp'))
- gradient: float32 [32768, 128], P(('feat', 'samp'))
The draws below stay inside these ranges and needn't reach their ends.
Inputs may be any that keep to these rules, and one draw needn't show every extreme that they name: `factor`: each entry's magnitude is below 40 * 32768 ** -0.4.
All inputs are finite; a program needn't handle non-finite values.
Results may differ from the reference program's by a relative error of at most 0.0074.
Values may be sent and summed in bfloat16 or wider, within the bound.
A program may use at most 64 MiB of HBM per device.

```python
import jax
import jax.numpy as jnp
from jax import lax

F = 32768
R = 128
ITERS = 2
SAMPLES = 6144


def draw_factor(key, part):
    key_base = jax.random.fold_in(key, 11)
    key_rows = jax.random.fold_in(key, 12)
    key_cols = jax.random.fold_in(key, 13)
    key_shared = jax.random.fold_in(key, 15)
    key_blocks = jax.random.fold_in(key, 16)
    base = jnp.clip(jax.random.normal(key_base, (F, R), jnp.float32), -3.5, 3.5)
    shared = jnp.clip(jax.random.normal(key_shared, (F, 1), jnp.float32), -3.5, 3.5)
    base = base + 0.4 * shared
    positions = jnp.arange(F, dtype=jnp.float32) / F
    rise = jnp.exp(jnp.log(3.0) * positions)
    row_scale = jnp.exp(jax.random.uniform(key_rows, (F,), jnp.float32, jnp.log(0.7), jnp.log(1.4)))
    col_scale = jnp.exp(jax.random.uniform(key_cols, (R,), jnp.float32, jnp.log(0.6), jnp.log(1.6)))
    block_index = jnp.arange(F, dtype=jnp.int32) * 32 // F
    block_table = jnp.exp(jax.random.uniform(key_blocks, (32, R), jnp.float32, jnp.log(0.6), jnp.log(1.67)))
    block_scale = jnp.take(block_table, block_index, axis=0)
    scale = 0.7 * float(F) ** (-0.4)
    return base * (scale * rise * row_scale)[:, None] * col_scale[None, :] * block_scale


def spiked(drawn, stream_key, source, target, parts, factor):
    def block_of(dim):
        return (jnp.arange(drawn.shape[dim]) // (drawn.shape[dim] // parts)).reshape((-1,) + (1,) * (drawn.ndim - 1 - dim))

    near = jax.random.permutation(stream_key, parts)[block_of(target)]
    second = (block_of(target) + parts // 2) % parts
    return jnp.where((block_of(source) == near) | (block_of(source) == second), factor * drawn, drawn)


def shard_levels(stream_key, extent, split, smallest, largest):
    factor_of, own = 1.0, jax.random.fold_in(stream_key, 6)
    for dim, parts in split:
        heights = jnp.exp(jax.random.uniform(jax.random.fold_in(own, dim), (parts,), jnp.float32, smallest / len(split), largest / len(split)))
        factor_of = factor_of * jnp.repeat(heights, extent[dim] // parts).reshape([-1 if axis == dim else 1 for axis in range(len(extent))])
    return factor_of


def noise_with(key, dims, deviation, limit, cuts, heavy, kind=jnp.bfloat16):
    array = deviation * jax.random.normal(key, dims, jnp.float32)
    if cuts:
        array = array * shard_levels(key, dims, cuts, -0.22, 0.18)
    return jnp.clip(spiked(array, jax.random.fold_in(key, 3), *heavy), -limit, limit).astype(kind)


def setup_inputs(seed: int = 0) -> dict:
    streams_of = jax.random.split(jax.random.key(seed), 3)
    samples = noise_with(streams_of[0], (SAMPLES, F), 1.0, 6.0, ((0, 16), (1, 2)), (0, 1, 16, 2.0))
    factor = draw_factor(jax.random.fold_in(streams_of[2], 71), 0)
    return dict(samples=samples, factor=factor)


step_size = 0.00025

def reference(samples, factor):
    current = factor
    gradient = jnp.zeros_like(factor)
    for step in range(ITERS):
        a_half = current.astype(jnp.bfloat16)
        proj = jnp.dot(samples, a_half, preferred_element_type=jnp.float32)
        square = (proj * proj).astype(jnp.bfloat16)
        moment = lax.dot_general(samples, square, (((0,), (0,)), ((), ())), preferred_element_type=jnp.float32)
        gram = lax.dot_general(current, current, (((0,), (0,)), ((), ())), precision=lax.Precision.HIGHEST, preferred_element_type=jnp.float32)
        model = jnp.dot(current, gram * gram, precision=lax.Precision.HIGHEST, preferred_element_type=jnp.float32)
        gradient = moment / jnp.sqrt(jnp.float32(SAMPLES)) - model
        current = current + step_size * gradient
    return (current, gradient)
```

```python
import jax
import jax.numpy as jnp
from jax import lax
from jax.sharding import PartitionSpec as P

ITERS = 2


step_size = 0.00025


def moment_owned(samples, square):
    partial_moment = lax.dot_general(
        samples, square, (((0,), (0,)), ((), ())), preferred_element_type=jnp.float32
    )
    return lax.psum_scatter(
        partial_moment.astype(jnp.bfloat16), "samp", scatter_dimension=0, tiled=True
    ).astype(jnp.float32)


def model_term(rows, gram):
    return jnp.dot(
        rows, gram * gram, precision=lax.Precision.HIGHEST, preferred_element_type=jnp.float32
    )


def local(samples, factor):
    count = samples.shape[0]
    total = count * lax.axis_size("samp")
    inv_root = 1.0 / jnp.sqrt(jnp.float32(total))
    current = factor
    gradient = jnp.zeros_like(factor)
    for step in range(ITERS):
        block = lax.all_gather(current.astype(jnp.bfloat16), "samp", axis=0, tiled=True)
        proj = jnp.dot(samples, block, preferred_element_type=jnp.float32)
        gram = lax.dot_general(
            block, block, (((0,), (0,)), ((), ())), preferred_element_type=jnp.float32
        )
        both = lax.psum(jnp.concatenate([proj, gram], axis=0), "feat")
        proj, gram = both[:count], both[count:]
        square = (proj * proj).astype(jnp.bfloat16)
        moment = moment_owned(samples, square)
        gradient = moment * inv_root - model_term(current, gram)
        current = current + step_size * gradient
    return (current, gradient)


def solution(mesh):
    in_specs = (P("samp", "feat"), P(("feat", "samp"), None))
    out_specs = (P(("feat", "samp"), None), P(("feat", "samp"), None))
    return jax.shard_map(local, mesh=mesh, in_specs=in_specs, out_specs=out_specs, check_vma=False)
```

```python
import functools

import jax
import jax.numpy as jnp
from jax import lax
from jax.experimental import pallas as pl
from jax.experimental.pallas import tpu as pltpu
from jax.sharding import PartitionSpec as P

ITERS = 2


step_size = 0.00025

MESH = pl.DeviceIdType.MESH
f32 = jnp.float32
bf16 = jnp.bfloat16


def kernel(
    L, nf, S, B, inv_root,
    samples, factor, out_cur, out_grad,
    sv, G, part, sq, frecv, acc, dbuf, ybuf, zbuf, drecv, yrecv, zrecv, model,
    s_in, g_recv, g_z, g_y, g_d, f_send, f_recv, d_send, d_recv, y_send, y_recv, z_send, z_recv,
):
    R = factor.shape[1]
    f = lax.axis_index("feat")
    s = lax.axis_index("samp")
    c, y, l = s % 2, (s // 2) % 2, s // 4
    below, above = l > 0, l < L - 1
    dev_d = (f, l * 4 + y * 2 + (1 - c))
    dev_y = (f, l * 4 + (1 - y) * 2 + c)
    dev_dn = (f, s - 4)
    dev_up = (f, s + 4)

    def dev_f(k):
        return (lax.rem(f + k, nf), s)

    load = pltpu.make_async_copy(samples, sv, s_in)
    load.start()

    barrier = pltpu.get_barrier_semaphore()

    def greet(dev):
        pl.semaphore_signal(barrier, inc=1, device_id=dev, device_id_type=MESH)

    greet(dev_d)
    greet(dev_y)
    for k in range(1, nf):
        greet(dev_f(k))

    @pl.when(below)
    def _():
        greet(dev_dn)

    @pl.when(above)
    def _():
        greet(dev_up)

    pl.semaphore_wait(barrier, nf + 1 + jnp.where(below, 1, 0) + jnp.where(above, 1, 0))

    def remote(src, dst, ssem, rsem, dev):
        return pltpu.make_async_remote_copy(
            src_ref=src, dst_ref=dst, send_sem=ssem, recv_sem=rsem,
            device_id=dev, device_id_type=MESH,
        )

    def block(p, core):
        return G.at[p, pl.ds(pl.multiple_of(core * B, B), B)]

    def g_copy(p, core, ssem, dev):
        ref = block(p, core)
        return remote(ref, ref, ssem, g_recv.at[p, core], dev)

    def g_to_dn(lb):
        return g_copy(lb * 2 + y, c, g_z.at[0, lb], dev_dn)

    def g_to_up(lb):
        return g_copy(lb * 2 + y, c, g_z.at[1, lb], dev_up)

    def g_to_y(lb):
        return g_copy(lb * 2 + y, c, g_y.at[lb], dev_y)

    def g_to_d(p):
        return g_copy(p, c, g_d.at[p], dev_d)

    def g_wait(p, core):
        g_copy(p, core, g_d.at[p], dev_d).wait_recv()

    def f_copy(it, k, which):
        rows = pl.ds(0, S) if which == 0 else pl.ds(S, R)
        return remote(
            part.at[rows], frecv.at[it, k - 1, rows],
            f_send.at[k - 1, which], f_recv.at[it, k - 1, which], dev_f(k),
        )

    def d_copy(p):
        return remote(dbuf.at[p], drecv.at[p], d_send.at[p], d_recv.at[p], dev_d)

    def y_copy(lb):
        return remote(ybuf.at[lb], yrecv.at[lb], y_send.at[lb], y_recv.at[lb], dev_y)

    def z_copy(way, lb):
        return remote(
            zbuf.at[lb], zrecv.at[way, lb], z_send.at[lb], z_recv.at[way, lb],
            dev_up if way == 0 else dev_dn,
        )

    def columns(p):
        return pl.ds(pl.multiple_of(p * (2 * B), 2 * B), 2 * B)

    def project(p):
        rows = G[p]
        part[0:S, :] += jnp.dot(sv[:, columns(p)], rows, preferred_element_type=f32)
        part[S : S + R, :] += lax.dot_general(
            rows, rows, (((0,), (0,)), ((), ())), preferred_element_type=f32
        )

    def inside(side, d):
        lb = l + side * d
        ok = (lb >= 0) & (lb < L) & (d >= 0)
        if side > 0:
            ok = ok & (d > 0)
        return lb, ok

    out_cur[...] = factor[...]

    def iteration(it, carry):
        G[l * 2 + y, pl.ds(pl.multiple_of(c * B, B), B), :] = out_cur[...].astype(bf16)

        @pl.when(below)
        def _():
            g_to_dn(l).start()

        @pl.when(above)
        def _():
            g_to_up(l).start()

        g_to_y(l).start()
        g_to_d(l * 2 + y).start()
        part[...] = jnp.zeros_like(part)

        @pl.when(it == 0)
        def _():
            load.wait()

        def gather_step(d, carry):
            for side in (-1, 1):
                lb, ok = inside(side, d)

                @pl.when(ok & (d > 0))
                def _():
                    g_wait(lb * 2 + y, c)
                    if side < 0:

                        @pl.when(above)
                        def _():
                            g_to_up(lb).start()
                    else:

                        @pl.when(below)
                        def _():
                            g_to_dn(lb).start()

                    g_to_y(lb).start()
                    g_to_d(lb * 2 + y).start()

            for side in (-1, 1):
                lb, ok = inside(side, d - 1)

                @pl.when(ok)
                def _():
                    g_wait(lb * 2 + 1 - y, c)
                    g_to_d(lb * 2 + 1 - y).start()

            for side in (-1, 1):
                lb, ok = inside(side, d)

                @pl.when(ok)
                def _():
                    g_wait(lb * 2 + y, 1 - c)
                    project(lb * 2 + y)

            for side in (-1, 1):
                lb, ok = inside(side, d - 1)

                @pl.when(ok)
                def _():
                    g_wait(lb * 2 + 1 - y, 1 - c)
                    project(lb * 2 + 1 - y)

            return carry

        lax.fori_loop(0, L + 1, gather_step, 0)

        for which in (0, 1):
            for k in range(1, nf):
                f_copy(it, k, which).start()

        def gather_sent(lb, carry):
            @pl.when((lb <= l) & above)
            def _():
                g_to_up(lb).wait_send()

            @pl.when((lb >= l) & below)
            def _():
                g_to_dn(lb).wait_send()

            g_to_y(lb).wait_send()
            g_to_d(lb * 2).wait_send()
            g_to_d(lb * 2 + 1).wait_send()
            return carry

        lax.fori_loop(0, L, gather_sent, 0)

        proj = part[0:S, :]
        for k in range(1, nf):
            f_copy(it, k, 0).wait_recv()
            proj = proj + frecv[it, k - 1, 0:S, :]
        sq[...] = (proj * proj).astype(bf16)

        def moment(p):
            m = lax.dot_general(
                sv[:, columns(p)], sq[...], (((0,), (0,)), ((), ())),
                preferred_element_type=f32,
            )
            lo, hi = m[:B], m[B:]
            acc[p] = jnp.where(c == 0, lo, hi)
            dbuf[p] = jnp.where(c == 0, hi, lo).astype(bf16)
            d_copy(p).start()

        def moment_step(i, carry):
            d = L - 1 - i
            for side in (-1, 1):
                lb, ok = inside(side, d)

                @pl.when(ok)
                def _():
                    p = lb * 2 + 1 - y
                    moment(p)
                    moment(lb * 2 + y)
                    d_copy(p).wait_recv()
                    ybuf[lb] = (acc[p] + drecv[p].astype(f32)).astype(bf16)
                    y_copy(lb).start()

            return carry

        lax.fori_loop(0, L, moment_step, 0)

        gram = part[S : S + R, :]
        for k in range(1, nf):
            f_copy(it, k, 1).wait_recv()
            gram = gram + frecv[it, k - 1, S : S + R, :]
        model[...] = jnp.dot(
            out_cur[...], gram * gram, precision=lax.Precision.HIGHEST,
            preferred_element_type=f32,
        )

        def line_step(i, carry):
            d = L - 1 - i
            for side in (-1, 1):
                lb, ok = inside(side, d)

                @pl.when(ok & (d > 0))
                def _():
                    p = lb * 2 + y
                    d_copy(p).wait_recv()
                    y_copy(lb).wait_recv()
                    way = 0 if side > 0 else 1
                    acc[p] = acc[p] + drecv[p].astype(f32) + yrecv[lb].astype(f32)

                    @pl.when(below if side > 0 else above)
                    def _():
                        z_copy(way, lb).wait_recv()
                        acc[p] = acc[p] + zrecv[way, lb].astype(f32)

                    zbuf[lb] = acc[p].astype(bf16)
                    z_copy(way, lb).start()

            return carry

        lax.fori_loop(0, L - 1, line_step, 0)

        own = l * 2 + y
        d_copy(own).wait_recv()
        y_copy(l).wait_recv()
        acc[own] = acc[own] + drecv[own].astype(f32) + yrecv[l].astype(f32)

        @pl.when(below)
        def _():
            z_copy(0, l).wait_recv()
            acc[own] = acc[own] + zrecv[0, l].astype(f32)

        @pl.when(above)
        def _():
            z_copy(1, l).wait_recv()
            acc[own] = acc[own] + zrecv[1, l].astype(f32)

        gradient = acc[own] * inv_root - model[...]
        out_grad[...] = gradient
        out_cur[...] = out_cur[...] + step_size * gradient

        def moment_sent(lb, carry):
            d_copy(lb * 2).wait_send()
            d_copy(lb * 2 + 1).wait_send()
            y_copy(lb).wait_send()

            @pl.when(lb != l)
            def _():
                z_copy(0, lb).wait_send()

            return carry

        lax.fori_loop(0, L, moment_sent, 0)
        for k in range(1, nf):
            for which in (0, 1):
                f_copy(it, k, which).wait_send()
        return carry

    lax.fori_loop(0, ITERS, iteration, 0)


def solution(mesh):
    nf, ns = mesh.shape["feat"], mesh.shape["samp"]
    L = ns // 4

    def local(samples, factor):
        S, W = samples.shape
        B, R = factor.shape
        inv_root = 1.0 / float(S * ns) ** 0.5
        DMA = pltpu.SemaphoreType.DMA
        V = pltpu.VMEM
        scratch = [
            V((S, W), bf16),
            V((2 * L, 2 * B, R), bf16),
            V((S + R, R), f32),
            V((S, R), bf16),
            V((ITERS, max(nf - 1, 1), S + R, R), f32),
            V((2 * L, B, R), f32),
            V((2 * L, B, R), bf16),
            V((L, B, R), bf16),
            V((L, B, R), bf16),
            V((2 * L, B, R), bf16),
            V((L, B, R), bf16),
            V((2, L, B, R), bf16),
            V((B, R), f32),
            DMA,
            DMA((2 * L, 2)),
            DMA((2, L)),
            DMA((L,)),
            DMA((2 * L,)),
            DMA((max(nf - 1, 1), 2)),
            DMA((ITERS, max(nf - 1, 1), 2)),
            DMA((2 * L,)),
            DMA((2 * L,)),
            DMA((L,)),
            DMA((L,)),
            DMA((L,)),
            DMA((2, L)),
        ]
        flops = ITERS * 4 * S * W * R
        return pl.pallas_call(
            functools.partial(kernel, L, nf, S, B, inv_root),
            out_shape=(
                jax.ShapeDtypeStruct((B, R), f32),
                jax.ShapeDtypeStruct((B, R), f32),
            ),
            in_specs=[
                pl.BlockSpec(memory_space=pl.ANY),
                pl.BlockSpec(memory_space=pltpu.VMEM),
            ],
            out_specs=(
                pl.BlockSpec(memory_space=pltpu.VMEM),
                pl.BlockSpec(memory_space=pltpu.VMEM),
            ),
            scratch_shapes=scratch,
            compiler_params=pltpu.CompilerParams(
                collective_id=0, has_side_effects=True, vmem_limit_bytes=56 * 2**20
            ),
            cost_estimate=pl.CostEstimate(
                flops=flops, bytes_accessed=2 * S * W, transcendentals=0
            ),
        )(samples, factor)

    in_specs = (P("samp", "feat"), P(("feat", "samp"), None))
    out_specs = (P(("feat", "samp"), None), P(("feat", "samp"), None))
    return jax.shard_map(local, mesh=mesh, in_specs=in_specs, out_specs=out_specs, check_vma=False)
```

```python
import functools

import jax
import jax.numpy as jnp
from jax import lax
from jax.experimental import pallas as pl
from jax.experimental.pallas import tpu as pltpu
from jax.sharding import PartitionSpec as P

ITERS = 2


step_size = 0.00025

MESH = pl.DeviceIdType.MESH
f32 = jnp.float32
bf16 = jnp.bfloat16


def kernel(
    L, nf, S, B, inv_root,
    samples, factor, out_cur, out_grad,
    sv, G, part, rest, rest_half, sq, frecv, frecv_half, frecv_gram, acc, dbuf, ybuf, zbuf, drecv, yrecv, zrecv, model,
    s_in, g_recv, g_z, g_y, g_d, f_send, f_recv, d_send, d_recv, y_send, y_recv, z_send, z_recv,
):
    R = factor.shape[1]
    f = lax.axis_index("feat")
    s = lax.axis_index("samp")
    c, y, l = s % 2, (s // 2) % 2, s // 4
    below, above = l > 0, l < L - 1
    dev_d = (f, l * 4 + y * 2 + (1 - c))
    dev_y = (f, l * 4 + (1 - y) * 2 + c)
    dev_dn = (f, s - 4)
    dev_up = (f, s + 4)

    def dev_f(k):
        return (lax.rem(f + k, nf), s)

    load = pltpu.make_async_copy(samples, sv, s_in)
    load.start()

    barrier = pltpu.get_barrier_semaphore()

    def greet(dev):
        pl.semaphore_signal(barrier, inc=1, device_id=dev, device_id_type=MESH)

    greet(dev_d)
    greet(dev_y)
    for k in range(1, nf):
        greet(dev_f(k))

    @pl.when(below)
    def _():
        greet(dev_dn)

    @pl.when(above)
    def _():
        greet(dev_up)

    pl.semaphore_wait(barrier, nf + 1 + jnp.where(below, 1, 0) + jnp.where(above, 1, 0))

    def remote(src, dst, ssem, rsem, dev):
        return pltpu.make_async_remote_copy(
            src_ref=src, dst_ref=dst, send_sem=ssem, recv_sem=rsem,
            device_id=dev, device_id_type=MESH,
        )

    Bh = B // 2
    halves = (0, 1)

    def half(h):
        return pl.ds(h * Bh, Bh)

    def g_copy(p, core, h, ssem, dev):
        ref = G.at[p, pl.ds(pl.multiple_of(core * B + h * Bh, Bh), Bh)]
        return remote(ref, ref, ssem, g_recv.at[p, core, h], dev)

    def g_to_dn(lb, h):
        return g_copy(lb * 2 + y, c, h, g_z.at[0, lb, h], dev_dn)

    def g_to_up(lb, h):
        return g_copy(lb * 2 + y, c, h, g_z.at[1, lb, h], dev_up)

    def g_to_y(lb, h):
        return g_copy(lb * 2 + y, c, h, g_y.at[lb, h], dev_y)

    def g_to_d(p, h):
        return g_copy(p, c, h, g_d.at[p, h], dev_d)

    def g_wait(p, core, h):
        g_copy(p, core, h, g_d.at[p, h], dev_d).wait_recv()

    def f_copy(it, k, which):
        src, dst = (
            (part, frecv), (rest_half, frecv_half), (rest.at[pl.ds(S, R)], frecv_gram)
        )[which]
        return remote(
            src, dst.at[it, k - 1],
            f_send.at[k - 1, which], f_recv.at[it, k - 1, which], dev_f(k),
        )

    def d_copy(p):
        return remote(dbuf.at[p], drecv.at[p], d_send.at[p], d_recv.at[p], dev_d)

    def y_copy(lb, h):
        return remote(
            ybuf.at[lb, half(h)], yrecv.at[lb, half(h)], y_send.at[lb, h], y_recv.at[lb, h], dev_y
        )

    def z_copy(way, lb, h):
        return remote(
            zbuf.at[lb, half(h)], zrecv.at[way, lb, half(h)],
            z_send.at[lb, h], z_recv.at[way, lb, h],
            dev_up if way == 0 else dev_dn,
        )

    def columns(p):
        return pl.ds(pl.multiple_of(p * (2 * B), 2 * B), 2 * B)

    def project(p, into):
        rows = G[p]
        into[0:S, :] += jnp.dot(sv[:, columns(p)], rows, preferred_element_type=f32)
        into[S : S + R, :] += lax.dot_general(
            rows, rows, (((0,), (0,)), ((), ())), preferred_element_type=f32
        )

    def inside(side, d):
        lb = l + side * d
        ok = (lb >= 0) & (lb < L) & (d >= 0)
        if side > 0:
            ok = ok & (d > 0)
        return lb, ok

    out_cur[...] = factor[...]

    def iteration(it, carry):
        G[l * 2 + y, pl.ds(pl.multiple_of(c * B, B), B), :] = out_cur[...].astype(bf16)

        for h in halves:

            @pl.when(below)
            def _():
                g_to_dn(l, h).start()

            @pl.when(above)
            def _():
                g_to_up(l, h).start()

            g_to_y(l, h).start()
            g_to_d(l * 2 + y, h).start()
        part[...] = jnp.zeros_like(part)
        rest[...] = jnp.zeros_like(rest)

        @pl.when(it == 0)
        def _():
            load.wait()

        def gather_step(d, into):
            for side in (-1, 1):
                lb, ok = inside(side, d)

                @pl.when(ok & (d > 0))
                def _():
                    for h in halves:
                        g_wait(lb * 2 + y, c, h)
                        if side < 0:

                            @pl.when(above)
                            def _():
                                g_to_up(lb, h).start()
                        else:

                            @pl.when(below)
                            def _():
                                g_to_dn(lb, h).start()

                        g_to_y(lb, h).start()
                        g_to_d(lb * 2 + y, h).start()

            for side in (-1, 1):
                lb, ok = inside(side, d - 1)

                @pl.when(ok)
                def _():
                    for h in halves:
                        g_wait(lb * 2 + 1 - y, c, h)
                        g_to_d(lb * 2 + 1 - y, h).start()

            for side in (-1, 1):
                lb, ok = inside(side, d)

                @pl.when(ok)
                def _():
                    for h in halves:
                        g_wait(lb * 2 + y, 1 - c, h)
                    project(lb * 2 + y, into)

            for side in (-1, 1):
                lb, ok = inside(side, d - 1)

                @pl.when(ok)
                def _():
                    for h in halves:
                        g_wait(lb * 2 + 1 - y, 1 - c, h)
                    project(lb * 2 + 1 - y, into)

        last = jnp.maximum(l, L - 1 - l) + 1

        def early_step(d, carry):
            gather_step(d, part)
            return carry

        lax.fori_loop(0, last, early_step, 0)
        for k in range(1, nf):
            f_copy(it, k, 0).start()
        gather_step(last, rest)
        rest_half[...] = rest[0:S, :].astype(bf16)
        for k in range(1, nf):
            f_copy(it, k, 1).start()
        for k in range(1, nf):
            f_copy(it, k, 2).start()

        def gather_sent(lb, carry):
            for h in halves:

                @pl.when((lb <= l) & above)
                def _():
                    g_to_up(lb, h).wait_send()

                @pl.when((lb >= l) & below)
                def _():
                    g_to_dn(lb, h).wait_send()

                g_to_y(lb, h).wait_send()
                g_to_d(lb * 2, h).wait_send()
                g_to_d(lb * 2 + 1, h).wait_send()
            return carry

        lax.fori_loop(0, L, gather_sent, 0)

        proj = part[0:S, :] + rest[0:S, :]
        for k in range(1, nf):
            f_copy(it, k, 0).wait_recv()
            f_copy(it, k, 1).wait_recv()
            proj = proj + (frecv[it, k - 1, 0:S, :] + frecv_half[it, k - 1].astype(f32))
        sq[...] = (proj * proj).astype(bf16)

        def moment(p):
            m = lax.dot_general(
                sv[:, columns(p)], sq[...], (((0,), (0,)), ((), ())),
                preferred_element_type=f32,
            )
            lo, hi = m[:B], m[B:]
            acc[p] = jnp.where(c == 0, lo, hi)
            dbuf[p] = jnp.where(c == 0, hi, lo).astype(bf16)
            d_copy(p).start()

        def moment_step(i, carry):
            d = L - 1 - i
            for side in (-1, 1):
                lb, ok = inside(side, d)

                @pl.when(ok)
                def _():
                    p = lb * 2 + 1 - y
                    moment(p)
                    moment(lb * 2 + y)
                    d_copy(p).wait_recv()
                    for h in halves:
                        own = acc[p, half(h)] + drecv[p, half(h)].astype(f32)
                        ybuf[lb, half(h)] = own.astype(bf16)
                        y_copy(lb, h).start()

            return carry

        lax.fori_loop(0, L, moment_step, 0)

        gram = part[S : S + R, :] + rest[S : S + R, :]
        for k in range(1, nf):
            f_copy(it, k, 2).wait_recv()
            gram = gram + (frecv[it, k - 1, S : S + R, :] + frecv_gram[it, k - 1])
        model[...] = jnp.dot(
            out_cur[...], gram * gram, precision=lax.Precision.HIGHEST,
            preferred_element_type=f32,
        )

        def line_step(i, carry):
            d = L - 1 - i
            for side in (-1, 1):
                lb, ok = inside(side, d)

                @pl.when(ok & (d > 0))
                def _():
                    p = lb * 2 + y
                    d_copy(p).wait_recv()
                    way = 0 if side > 0 else 1
                    for h in halves:
                        y_copy(lb, h).wait_recv()
                        acc[p, half(h)] = (
                            acc[p, half(h)] + drecv[p, half(h)].astype(f32)
                            + yrecv[lb, half(h)].astype(f32)
                        )

                        @pl.when(below if side > 0 else above)
                        def _():
                            z_copy(way, lb, h).wait_recv()
                            acc[p, half(h)] = acc[p, half(h)] + zrecv[way, lb, half(h)].astype(f32)

                        zbuf[lb, half(h)] = acc[p, half(h)].astype(bf16)
                        z_copy(way, lb, h).start()

            return carry

        lax.fori_loop(0, L - 1, line_step, 0)

        own = l * 2 + y
        d_copy(own).wait_recv()
        for h in halves:
            y_copy(l, h).wait_recv()
        acc[own] = acc[own] + drecv[own].astype(f32) + yrecv[l].astype(f32)

        @pl.when(below)
        def _():
            for h in halves:
                z_copy(0, l, h).wait_recv()
            acc[own] = acc[own] + zrecv[0, l].astype(f32)

        @pl.when(above)
        def _():
            for h in halves:
                z_copy(1, l, h).wait_recv()
            acc[own] = acc[own] + zrecv[1, l].astype(f32)

        @pl.when(it < ITERS - 1)
        def _():
            gradient = acc[own] * inv_root - model[...]
            out_cur[...] = out_cur[...] + step_size * gradient

        @pl.when(it == ITERS - 1)
        def _():
            out_grad[...] = acc[own] - model[...] * (1.0 / inv_root)

        def moment_sent(lb, carry):
            d_copy(lb * 2).wait_send()
            d_copy(lb * 2 + 1).wait_send()
            for h in halves:
                y_copy(lb, h).wait_send()

            @pl.when(lb != l)
            def _():
                for h in halves:
                    z_copy(0, lb, h).wait_send()

            return carry

        lax.fori_loop(0, L, moment_sent, 0)
        for k in range(1, nf):
            for which in (0, 1, 2):
                f_copy(it, k, which).wait_send()
        return carry

    lax.fori_loop(0, ITERS, iteration, 0)


def solution(mesh):
    nf, ns = mesh.shape["feat"], mesh.shape["samp"]
    L = ns // 4

    def local(samples, factor):
        S, W = samples.shape
        B, R = factor.shape
        inv_root = 1.0 / float(S * ns) ** 0.5
        DMA = pltpu.SemaphoreType.DMA
        V = pltpu.VMEM
        peers = max(nf - 1, 1)
        scratch = [
            V((S, W), bf16),
            V((2 * L, 2 * B, R), bf16),
            V((S + R, R), f32),
            V((S + R, R), f32),
            V((S, R), bf16),
            V((S, R), bf16),
            V((ITERS, peers, S + R, R), f32),
            V((ITERS, peers, S, R), bf16),
            V((ITERS, peers, R, R), f32),
            V((2 * L, B, R), f32),
            V((2 * L, B, R), bf16),
            V((L, B, R), bf16),
            V((L, B, R), bf16),
            V((2 * L, B, R), bf16),
            V((L, B, R), bf16),
            V((2, L, B, R), bf16),
            V((B, R), f32),
            DMA,
            DMA((2 * L, 2, 2)),
            DMA((2, L, 2)),
            DMA((L, 2)),
            DMA((2 * L, 2)),
            DMA((peers, 3)),
            DMA((ITERS, peers, 3)),
            DMA((2 * L,)),
            DMA((2 * L,)),
            DMA((L, 2)),
            DMA((L, 2)),
            DMA((L, 2)),
            DMA((2, L, 2)),
        ]
        flops = ITERS * 4 * S * W * R
        previous, scaled = pl.pallas_call(
            functools.partial(kernel, L, nf, S, B, inv_root),
            out_shape=(
                jax.ShapeDtypeStruct((B, R), f32),
                jax.ShapeDtypeStruct((B, R), f32),
            ),
            in_specs=[
                pl.BlockSpec(memory_space=pl.ANY),
                pl.BlockSpec(memory_space=pltpu.VMEM),
            ],
            out_specs=(
                pl.BlockSpec(memory_space=pltpu.VMEM),
                pl.BlockSpec(memory_space=pltpu.VMEM),
            ),
            scratch_shapes=scratch,
            compiler_params=pltpu.CompilerParams(
                collective_id=0, has_side_effects=True, vmem_limit_bytes=56 * 2**20
            ),
            cost_estimate=pl.CostEstimate(
                flops=flops, bytes_accessed=2 * S * W, transcendentals=0
            ),
        )(samples, factor)
        gradient = scaled * inv_root
        return (previous + step_size * gradient, gradient)

    in_specs = (P("samp", "feat"), P(("feat", "samp"), None))
    out_specs = (P(("feat", "samp"), None), P(("feat", "samp"), None))
    return jax.shard_map(local, mesh=mesh, in_specs=in_specs, out_specs=out_specs, check_vma=False)
```

```python
import functools

import jax
import jax.numpy as jnp
from jax import lax
from jax.experimental import pallas as pl
from jax.experimental.pallas import tpu as pltpu
from jax.sharding import PartitionSpec as P

ITERS = 2


step_size = 0.00025

MESH = pl.DeviceIdType.MESH
f32 = jnp.float32
bf16 = jnp.bfloat16


def kernel(
    L, nf, S, B, inv_root,
    samples, factor, out_cur, out_grad,
    sv, G, part, rest, rest_half, sq, frecv, frecv_half, frecv_gram, acc, dbuf, ybuf, zbuf, drecv, yrecv, zrecv, model,
    s_in, g_recv, g_z, g_y, g_d, f_send, f_recv, d_send, d_recv, y_send, y_recv, z_send, z_recv,
    xbuf, xrecv, x_send, x_recv,
):
    R = factor.shape[1]
    f = lax.axis_index("feat")
    s = lax.axis_index("samp")
    c, y, l = s % 2, (s // 2) % 2, s // 4
    below, above = l > 0, l < L - 1
    dev_d = (f, l * 4 + y * 2 + (1 - c))
    dev_y = (f, l * 4 + (1 - y) * 2 + c)
    spread = L >= 4 and L % 2 == 0
    n = l + 1 - 2 * (l % 2) if spread else -1
    dev_n = (f, n * 4 + y * 2 + c)
    relay_step = jnp.maximum(jnp.where(l % 2 == 0, l, L - 1 - l), 1)
    dev_dn = (f, s - 4)
    dev_up = (f, s + 4)

    def dev_f(k):
        return (lax.rem(f + k, nf), s)

    load = pltpu.make_async_copy(samples, sv, s_in)
    load.start()

    barrier = pltpu.get_barrier_semaphore()

    def greet(dev):
        pl.semaphore_signal(barrier, inc=1, device_id=dev, device_id_type=MESH)

    greet(dev_d)
    greet(dev_y)
    for k in range(1, nf):
        greet(dev_f(k))

    @pl.when(below)
    def _():
        greet(dev_dn)

    @pl.when(above)
    def _():
        greet(dev_up)

    pl.semaphore_wait(barrier, nf + 1 + jnp.where(below, 1, 0) + jnp.where(above, 1, 0))

    def remote(src, dst, ssem, rsem, dev):
        return pltpu.make_async_remote_copy(
            src_ref=src, dst_ref=dst, send_sem=ssem, recv_sem=rsem,
            device_id=dev, device_id_type=MESH,
        )

    Bh = B // 2
    halves = (0, 1)

    def half(h):
        return pl.ds(h * Bh, Bh)

    def g_copy(p, core, h, ssem, dev):
        ref = G.at[p, pl.ds(pl.multiple_of(core * B + h * Bh, Bh), Bh)]
        return remote(ref, ref, ssem, g_recv.at[p, core, h], dev)

    def g_to_dn(lb, h):
        return g_copy(lb * 2 + y, c, h, g_z.at[0, lb, h], dev_dn)

    def g_to_up(lb, h):
        return g_copy(lb * 2 + y, c, h, g_z.at[1, lb, h], dev_up)

    def g_to_y(lb, h):
        return g_copy(lb * 2 + y, c, h, g_y.at[lb, h], dev_y)

    def g_to_d(p, h):
        return g_copy(p, c, h, g_d.at[p, h], dev_d)

    def g_relay():
        return g_copy(l * 2 + 1 - y, c, 1, g_z.at[1 - l % 2, n, 1], dev_n)

    def x_copy():
        return remote(xbuf, xrecv, x_send, x_recv, dev_n)

    def g_wait(p, core, h):
        g_copy(p, core, h, g_d.at[p, h], dev_d).wait_recv()

    def f_copy(it, k, which):
        src, dst = (
            (part, frecv), (rest_half, frecv_half), (rest.at[pl.ds(S, R)], frecv_gram)
        )[which]
        return remote(
            src, dst.at[it, k - 1],
            f_send.at[k - 1, which], f_recv.at[it, k - 1, which], dev_f(k),
        )

    def d_copy(p):
        return remote(dbuf.at[p], drecv.at[p], d_send.at[p], d_recv.at[p], dev_d)

    def y_copy(lb, h):
        return remote(
            ybuf.at[lb, half(h)], yrecv.at[lb, half(h)], y_send.at[lb, h], y_recv.at[lb, h], dev_y
        )

    def z_copy(way, lb, h):
        return remote(
            zbuf.at[lb, half(h)], zrecv.at[way, lb, half(h)],
            z_send.at[lb, h], z_recv.at[way, lb, h],
            dev_up if way == 0 else dev_dn,
        )

    def columns(p):
        return pl.ds(pl.multiple_of(p * (2 * B), 2 * B), 2 * B)

    def project(p, into):
        rows = G[p]
        into[0:S, :] += jnp.dot(sv[:, columns(p)], rows, preferred_element_type=f32)
        into[S : S + R, :] += lax.dot_general(
            rows, rows, (((0,), (0,)), ((), ())), preferred_element_type=f32
        )

    def inside(side, d):
        lb = l + side * d
        ok = (lb >= 0) & (lb < L) & (d >= 0)
        if side > 0:
            ok = ok & (d > 0)
        return lb, ok

    out_cur[...] = factor[...]

    def iteration(it, carry):
        G[l * 2 + y, pl.ds(pl.multiple_of(c * B, B), B), :] = out_cur[...].astype(bf16)

        for h in halves:

            @pl.when(below)
            def _():
                g_to_dn(l, h).start()

            @pl.when(above)
            def _():
                g_to_up(l, h).start()

            g_to_y(l, h).start()
            g_to_d(l * 2 + y, h).start()
        part[...] = jnp.zeros_like(part)
        rest[...] = jnp.zeros_like(rest)

        @pl.when(it == 0)
        def _():
            load.wait()

        def gather_step(d, into, final=False):
            for side in (-1, 1):
                lb, ok = inside(side, d)

                @pl.when(ok & (d > 0))
                def _():
                    for h in halves:
                        g_wait(lb * 2 + y, c, h)
                        if side < 0:

                            @pl.when(above)
                            def _():
                                g_to_up(lb, h).start()
                        else:

                            @pl.when(below)
                            def _():
                                g_to_dn(lb, h).start()

                        if h == 0:
                            g_to_y(lb, h).start()
                        else:

                            @pl.when(lb != n)
                            def _():
                                g_to_y(lb, h).start()

                        g_to_d(lb * 2 + y, h).start()

            for side in (-1, 1):
                lb, ok = inside(side, d - 1)

                @pl.when(ok)
                def _():
                    g_wait(lb * 2 + 1 - y, c, 0)
                    g_to_d(lb * 2 + 1 - y, 0).start()

                    @pl.when(lb != n)
                    def _():
                        g_wait(lb * 2 + 1 - y, c, 1)
                        g_to_d(lb * 2 + 1 - y, 1).start()

            if spread:

                @pl.when(d == relay_step)
                def _():
                    g_relay().start()

                if final:
                    g_wait(n * 2 + 1 - y, c, 1)
                    g_to_d(n * 2 + 1 - y, 1).start()

            for side in (-1, 1):
                lb, ok = inside(side, d)

                @pl.when(ok)
                def _():
                    for h in halves:
                        g_wait(lb * 2 + y, 1 - c, h)
                    project(lb * 2 + y, into)

            for side in (-1, 1):
                lb, ok = inside(side, d - 1)

                @pl.when(ok & (lb != n))
                def _():
                    for h in halves:
                        g_wait(lb * 2 + 1 - y, 1 - c, h)
                    project(lb * 2 + 1 - y, into)

            if spread and final:
                for h in halves:
                    g_wait(n * 2 + 1 - y, 1 - c, h)
                project(n * 2 + 1 - y, into)

        last = jnp.maximum(l, L - 1 - l) + 1

        def early_step(d, carry):
            gather_step(d, part)
            return carry

        lax.fori_loop(0, last, early_step, 0)
        for k in range(1, nf):
            f_copy(it, k, 0).start()
        gather_step(last, rest, final=True)
        rest_half[...] = rest[0:S, :].astype(bf16)
        for k in range(1, nf):
            f_copy(it, k, 1).start()
        for k in range(1, nf):
            f_copy(it, k, 2).start()

        def gather_sent(lb, carry):
            for h in halves:

                @pl.when((lb <= l) & above)
                def _():
                    g_to_up(lb, h).wait_send()

                @pl.when((lb >= l) & below)
                def _():
                    g_to_dn(lb, h).wait_send()

                @pl.when((lb != n) | (h == 0))
                def _():
                    g_to_y(lb, h).wait_send()

                g_to_d(lb * 2, h).wait_send()
                g_to_d(lb * 2 + 1, h).wait_send()
            return carry

        lax.fori_loop(0, L, gather_sent, 0)
        if spread:
            g_relay().wait_send()

        proj = part[0:S, :] + rest[0:S, :]
        for k in range(1, nf):
            f_copy(it, k, 0).wait_recv()
            f_copy(it, k, 1).wait_recv()
            proj = proj + (frecv[it, k - 1, 0:S, :] + frecv_half[it, k - 1].astype(f32))
        sq[...] = (proj * proj).astype(bf16)

        def moment(p):
            m = lax.dot_general(
                sv[:, columns(p)], sq[...], (((0,), (0,)), ((), ())),
                preferred_element_type=f32,
            )
            lo, hi = m[:B], m[B:]
            acc[p] = jnp.where(c == 0, lo, hi)
            dbuf[p] = jnp.where(c == 0, hi, lo).astype(bf16)
            d_copy(p).start()

        def moment_step(i, carry):
            d = L - 1 - i
            for side in (-1, 1):
                lb, ok = inside(side, d)

                @pl.when(ok)
                def _():
                    p = lb * 2 + 1 - y

                    def half_sum(h):
                        return acc[p, half(h)] + drecv[p, half(h)].astype(f32)

                    @pl.when(lb != n)
                    def _():
                        moment(p)

                    moment(lb * 2 + y)

                    @pl.when(lb != n)
                    def _():
                        d_copy(p).wait_recv()

                    ybuf[lb, half(0)] = half_sum(0).astype(bf16)
                    y_copy(lb, 0).start()

                    @pl.when((lb != n) & (lb != l) if spread else lb >= 0)
                    def _():
                        ybuf[lb, half(1)] = half_sum(1).astype(bf16)
                        y_copy(lb, 1).start()

                    if spread and side < 0:

                        @pl.when(lb == l)
                        def _():
                            x_copy().wait_recv()
                            ybuf[lb, half(1)] = (half_sum(1) + xrecv[...].astype(f32)).astype(bf16)
                            y_copy(lb, 1).start()

            if spread:

                @pl.when(i == 0)
                def _():
                    p = n * 2 + 1 - y
                    d_copy(p).wait_recv()
                    xbuf[...] = (acc[p, half(1)] + drecv[p, half(1)].astype(f32)).astype(bf16)
                    x_copy().start()

            return carry

        if spread:
            moment(n * 2 + 1 - y)
        lax.fori_loop(0, L, moment_step, 0)

        gram = part[S : S + R, :] + rest[S : S + R, :]
        for k in range(1, nf):
            f_copy(it, k, 2).wait_recv()
            gram = gram + (frecv[it, k - 1, S : S + R, :] + frecv_gram[it, k - 1])
        model[...] = jnp.dot(
            out_cur[...], gram * gram, precision=lax.Precision.HIGHEST,
            preferred_element_type=f32,
        )

        def line_step(i, carry):
            d = L - 1 - i
            for side in (-1, 1):
                lb, ok = inside(side, d)

                @pl.when(ok & (d > 0))
                def _():
                    p = lb * 2 + y
                    d_copy(p).wait_recv()
                    way = 0 if side > 0 else 1
                    for h in halves:
                        acc[p, half(h)] = acc[p, half(h)] + drecv[p, half(h)].astype(f32)

                        @pl.when((lb != n) | (h == 0))
                        def _():
                            y_copy(lb, h).wait_recv()
                            acc[p, half(h)] = acc[p, half(h)] + yrecv[lb, half(h)].astype(f32)

                        @pl.when(below if side > 0 else above)
                        def _():
                            z_copy(way, lb, h).wait_recv()
                            acc[p, half(h)] = acc[p, half(h)] + zrecv[way, lb, half(h)].astype(f32)

                        zbuf[lb, half(h)] = acc[p, half(h)].astype(bf16)
                        z_copy(way, lb, h).start()

            return carry

        lax.fori_loop(0, L - 1, line_step, 0)

        own = l * 2 + y
        d_copy(own).wait_recv()
        for h in halves:
            y_copy(l, h).wait_recv()
        acc[own] = acc[own] + drecv[own].astype(f32) + yrecv[l].astype(f32)

        @pl.when(below)
        def _():
            for h in halves:
                z_copy(0, l, h).wait_recv()
            acc[own] = acc[own] + zrecv[0, l].astype(f32)

        @pl.when(above)
        def _():
            for h in halves:
                z_copy(1, l, h).wait_recv()
            acc[own] = acc[own] + zrecv[1, l].astype(f32)

        @pl.when(it < ITERS - 1)
        def _():
            gradient = acc[own] * inv_root - model[...]
            out_cur[...] = out_cur[...] + step_size * gradient

        @pl.when(it == ITERS - 1)
        def _():
            out_grad[...] = acc[own] - model[...] * (1.0 / inv_root)

        def moment_sent(lb, carry):
            d_copy(lb * 2).wait_send()
            d_copy(lb * 2 + 1).wait_send()
            y_copy(lb, 0).wait_send()

            @pl.when(lb != n)
            def _():
                y_copy(lb, 1).wait_send()

            @pl.when(lb != l)
            def _():
                for h in halves:
                    z_copy(0, lb, h).wait_send()

            return carry

        lax.fori_loop(0, L, moment_sent, 0)
        if spread:
            x_copy().wait_send()
        for k in range(1, nf):
            for which in (0, 1, 2):
                f_copy(it, k, which).wait_send()
        return carry

    lax.fori_loop(0, ITERS, iteration, 0)


def solution(mesh):
    nf, ns = mesh.shape["feat"], mesh.shape["samp"]
    L = ns // 4

    def local(samples, factor):
        S, W = samples.shape
        B, R = factor.shape
        inv_root = 1.0 / float(S * ns) ** 0.5
        DMA = pltpu.SemaphoreType.DMA
        V = pltpu.VMEM
        peers = max(nf - 1, 1)
        scratch = [
            V((S, W), bf16),
            V((2 * L, 2 * B, R), bf16),
            V((S + R, R), f32),
            V((S + R, R), f32),
            V((S, R), bf16),
            V((S, R), bf16),
            V((ITERS, peers, S + R, R), f32),
            V((ITERS, peers, S, R), bf16),
            V((ITERS, peers, R, R), f32),
            V((2 * L, B, R), f32),
            V((2 * L, B, R), bf16),
            V((L, B, R), bf16),
            V((L, B, R), bf16),
            V((2 * L, B, R), bf16),
            V((L, B, R), bf16),
            V((2, L, B, R), bf16),
            V((B, R), f32),
            DMA,
            DMA((2 * L, 2, 2)),
            DMA((2, L, 2)),
            DMA((L, 2)),
            DMA((2 * L, 2)),
            DMA((peers, 3)),
            DMA((ITERS, peers, 3)),
            DMA((2 * L,)),
            DMA((2 * L,)),
            DMA((L, 2)),
            DMA((L, 2)),
            DMA((L, 2)),
            DMA((2, L, 2)),
            V((B // 2, R), bf16),
            V((B // 2, R), bf16),
            DMA,
            DMA,
        ]
        flops = ITERS * 4 * S * W * R
        previous, scaled = pl.pallas_call(
            functools.partial(kernel, L, nf, S, B, inv_root),
            out_shape=(
                jax.ShapeDtypeStruct((B, R), f32),
                jax.ShapeDtypeStruct((B, R), f32),
            ),
            in_specs=[
                pl.BlockSpec(memory_space=pl.ANY),
                pl.BlockSpec(memory_space=pltpu.VMEM),
            ],
            out_specs=(
                pl.BlockSpec(memory_space=pltpu.VMEM),
                pl.BlockSpec(memory_space=pltpu.VMEM),
            ),
            scratch_shapes=scratch,
            compiler_params=pltpu.CompilerParams(
                collective_id=0, has_side_effects=True, vmem_limit_bytes=56 * 2**20
            ),
            cost_estimate=pl.CostEstimate(
                flops=flops, bytes_accessed=2 * S * W, transcendentals=0
            ),
        )(samples, factor)
        gradient = scaled * inv_root
        return (previous + step_size * gradient, gradient)

    in_specs = (P("samp", "feat"), P(("feat", "samp"), None))
    out_specs = (P(("feat", "samp"), None), P(("feat", "samp"), None))
    return jax.shard_map(local, mesh=mesh, in_specs=in_specs, out_specs=out_specs, check_vma=False)
```

```python
import functools

import jax
import jax.numpy as jnp
from jax import lax
from jax.experimental import pallas as pl
from jax.experimental.pallas import tpu as pltpu
from jax.sharding import PartitionSpec as P

ITERS = 2


step_size = 0.00025

MESH = pl.DeviceIdType.MESH
f32 = jnp.float32
bf16 = jnp.bfloat16


def kernel(
    L, nf, S, B, inv_root,
    samples, factor, out_cur, out_grad,
    sv, G, part, rest, rest_half, sq, frecv, frecv_half, frecv_gram, acc, dbuf, ybuf, zbuf, drecv, yrecv, zrecv, model,
    s_in, g_recv, g_z, g_y, g_d, f_send, f_recv, d_send, d_recv, y_send, y_recv, z_send, z_recv,
):
    R = factor.shape[1]
    f = lax.axis_index("feat")
    s = lax.axis_index("samp")
    c, y, l = s % 2, (s // 2) % 2, s // 4
    below, above = l > 0, l < L - 1
    dev_d = (f, l * 4 + y * 2 + (1 - c))
    dev_y = (f, l * 4 + (1 - y) * 2 + c)
    dev_dn = (f, s - 4)
    dev_up = (f, s + 4)

    def dev_f(k):
        return (lax.rem(f + k, nf), s)

    load = pltpu.make_async_copy(samples, sv, s_in)
    load.start()

    barrier = pltpu.get_barrier_semaphore()

    def greet(dev):
        pl.semaphore_signal(barrier, inc=1, device_id=dev, device_id_type=MESH)

    greet(dev_d)
    greet(dev_y)
    for k in range(1, nf):
        greet(dev_f(k))

    @pl.when(below)
    def _():
        greet(dev_dn)

    @pl.when(above)
    def _():
        greet(dev_up)

    pl.semaphore_wait(barrier, nf + 1 + jnp.where(below, 1, 0) + jnp.where(above, 1, 0))

    def remote(src, dst, ssem, rsem, dev):
        return pltpu.make_async_remote_copy(
            src_ref=src, dst_ref=dst, send_sem=ssem, recv_sem=rsem,
            device_id=dev, device_id_type=MESH,
        )

    Bh = B // 2
    halves = (0, 1)

    def half(h):
        return pl.ds(h * Bh, Bh)

    def g_copy(p, core, h, ssem, dev):
        ref = G.at[p, pl.ds(pl.multiple_of(core * B + h * Bh, Bh), Bh)]
        return remote(ref, ref, ssem, g_recv.at[p, core, h], dev)

    def g_to_dn(lb, h):
        return g_copy(lb * 2 + y, c, h, g_z.at[0, lb, h], dev_dn)

    def g_to_up(lb, h):
        return g_copy(lb * 2 + y, c, h, g_z.at[1, lb, h], dev_up)

    def g_to_y(lb, h):
        return g_copy(lb * 2 + y, c, h, g_y.at[lb, h], dev_y)

    def g_to_d(p, h):
        return g_copy(p, c, h, g_d.at[p, h], dev_d)

    def g_wait(p, core, h):
        g_copy(p, core, h, g_d.at[p, h], dev_d).wait_recv()

    def f_copy(it, k, which):
        src, dst = (
            (part, frecv), (rest_half, frecv_half), (rest.at[pl.ds(S, R)], frecv_gram)
        )[which]
        return remote(
            src, dst.at[it, k - 1],
            f_send.at[k - 1, which], f_recv.at[it, k - 1, which], dev_f(k),
        )

    def d_copy(p):
        return remote(dbuf.at[p], drecv.at[p], d_send.at[p], d_recv.at[p], dev_d)

    def y_copy(lb, h):
        return remote(
            ybuf.at[lb, half(h)], yrecv.at[lb, half(h)], y_send.at[lb, h], y_recv.at[lb, h], dev_y
        )

    def z_copy(way, lb, h):
        return remote(
            zbuf.at[lb, half(h)], zrecv.at[way, lb, half(h)],
            z_send.at[lb, h], z_recv.at[way, lb, h],
            dev_up if way == 0 else dev_dn,
        )

    def columns(p):
        return pl.ds(pl.multiple_of(p * (2 * B), 2 * B), 2 * B)

    def project(p, into):
        rows = G[p]
        into[0:S, :] += jnp.dot(sv[:, columns(p)], rows, preferred_element_type=f32)
        into[S : S + R, :] += lax.dot_general(
            rows, rows, (((0,), (0,)), ((), ())), preferred_element_type=f32
        )

    def inside(side, d):
        lb = l + side * d
        ok = (lb >= 0) & (lb < L) & (d >= 0)
        if side > 0:
            ok = ok & (d > 0)
        return lb, ok

    out_cur[...] = factor[...]

    def iteration(it, carry):
        G[l * 2 + y, pl.ds(pl.multiple_of(c * B, B), B), :] = out_cur[...].astype(bf16)

        for h in halves:

            @pl.when(below)
            def _():
                g_to_dn(l, h).start()

            @pl.when(above)
            def _():
                g_to_up(l, h).start()

            g_to_y(l, h).start()
            g_to_d(l * 2 + y, h).start()
        part[...] = jnp.zeros_like(part)
        rest[...] = jnp.zeros_like(rest)

        @pl.when(it == 0)
        def _():
            load.wait()

        def gather_step(d, into):
            for side in (-1, 1):
                lb, ok = inside(side, d)

                @pl.when(ok & (d > 0))
                def _():
                    for h in halves:
                        g_wait(lb * 2 + y, c, h)
                        if side < 0:

                            @pl.when(above)
                            def _():
                                g_to_up(lb, h).start()
                        else:

                            @pl.when(below)
                            def _():
                                g_to_dn(lb, h).start()

                        g_to_y(lb, h).start()
                        g_to_d(lb * 2 + y, h).start()

            for side in (-1, 1):
                lb, ok = inside(side, d - 1)

                @pl.when(ok)
                def _():
                    for h in halves:
                        g_wait(lb * 2 + 1 - y, c, h)
                        g_to_d(lb * 2 + 1 - y, h).start()

            for side in (-1, 1):
                lb, ok = inside(side, d)

                @pl.when(ok)
                def _():
                    for h in halves:
                        g_wait(lb * 2 + y, 1 - c, h)
                    project(lb * 2 + y, into)

            for side in (-1, 1):
                lb, ok = inside(side, d - 1)

                @pl.when(ok)
                def _():
                    for h in halves:
                        g_wait(lb * 2 + 1 - y, 1 - c, h)
                    project(lb * 2 + 1 - y, into)

        last = jnp.maximum(l, L - 1 - l) + 1

        def early_step(d, carry):
            gather_step(d, part)
            return carry

        lax.fori_loop(0, last, early_step, 0)
        for k in range(1, nf):
            f_copy(it, k, 0).start()
        gather_step(last, rest)
        rest_half[...] = rest[0:S, :].astype(bf16)
        for k in range(1, nf):
            f_copy(it, k, 1).start()
        for k in range(1, nf):
            f_copy(it, k, 2).start()

        def gather_sent(lb, carry):
            for h in halves:

                @pl.when((lb <= l) & above)
                def _():
                    g_to_up(lb, h).wait_send()

                @pl.when((lb >= l) & below)
                def _():
                    g_to_dn(lb, h).wait_send()

                g_to_y(lb, h).wait_send()
                g_to_d(lb * 2, h).wait_send()
                g_to_d(lb * 2 + 1, h).wait_send()
            return carry

        lax.fori_loop(0, L, gather_sent, 0)

        proj = part[0:S, :] + rest[0:S, :]
        for k in range(1, nf):
            f_copy(it, k, 0).wait_recv()
            f_copy(it, k, 1).wait_recv()
            proj = proj + (frecv[it, k - 1, 0:S, :] + frecv_half[it, k - 1].astype(f32))
        sq[...] = (proj * proj).astype(bf16)

        def moment(p):
            m = lax.dot_general(
                sv[:, columns(p)], sq[...], (((0,), (0,)), ((), ())),
                preferred_element_type=f32,
            )
            lo, hi = m[:B], m[B:]
            acc[p] = jnp.where(c == 0, lo, hi)
            dbuf[p] = jnp.where(c == 0, hi, lo).astype(bf16)
            d_copy(p).start()

        def line_step(i, carry):
            d = L - 1 - i
            for side in (-1, 1):
                lb, ok = inside(side, d)

                @pl.when(ok & (d > 0))
                def _():
                    p = lb * 2 + y
                    d_copy(p).wait_recv()
                    way = 0 if side > 0 else 1
                    for h in halves:
                        y_copy(lb, h).wait_recv()
                        acc[p, half(h)] = (
                            acc[p, half(h)] + drecv[p, half(h)].astype(f32)
                            + yrecv[lb, half(h)].astype(f32)
                        )

                        @pl.when(below if side > 0 else above)
                        def _():
                            z_copy(way, lb, h).wait_recv()
                            acc[p, half(h)] = acc[p, half(h)] + zrecv[way, lb, half(h)].astype(f32)

                        zbuf[lb, half(h)] = acc[p, half(h)].astype(bf16)
                        z_copy(way, lb, h).start()

            return carry

        def moment_step(i, carry):
            d = L - 1 - i
            for side in (-1, 1):
                lb, ok = inside(side, d)

                @pl.when(ok)
                def _():
                    p = lb * 2 + 1 - y
                    moment(p)
                    moment(lb * 2 + y)
                    d_copy(p).wait_recv()
                    for h in halves:
                        own = acc[p, half(h)] + drecv[p, half(h)].astype(f32)
                        ybuf[lb, half(h)] = own.astype(bf16)
                        y_copy(lb, h).start()

            @pl.when(i > 0)
            def _():
                line_step(i - 1, 0)

            return carry

        lax.fori_loop(0, L, moment_step, 0)

        gram = part[S : S + R, :] + rest[S : S + R, :]
        for k in range(1, nf):
            f_copy(it, k, 2).wait_recv()
            gram = gram + (frecv[it, k - 1, S : S + R, :] + frecv_gram[it, k - 1])
        model[...] = jnp.dot(
            out_cur[...], gram * gram, precision=lax.Precision.HIGHEST,
            preferred_element_type=f32,
        )

        own = l * 2 + y
        d_copy(own).wait_recv()
        for h in halves:
            y_copy(l, h).wait_recv()
        acc[own] = acc[own] + drecv[own].astype(f32) + yrecv[l].astype(f32)

        @pl.when(below)
        def _():
            for h in halves:
                z_copy(0, l, h).wait_recv()
            acc[own] = acc[own] + zrecv[0, l].astype(f32)

        @pl.when(above)
        def _():
            for h in halves:
                z_copy(1, l, h).wait_recv()
            acc[own] = acc[own] + zrecv[1, l].astype(f32)

        @pl.when(it < ITERS - 1)
        def _():
            gradient = acc[own] * inv_root - model[...]
            out_cur[...] = out_cur[...] + step_size * gradient

        @pl.when(it == ITERS - 1)
        def _():
            out_grad[...] = acc[own] - model[...] * (1.0 / inv_root)

        def moment_sent(lb, carry):
            d_copy(lb * 2).wait_send()
            d_copy(lb * 2 + 1).wait_send()
            for h in halves:
                y_copy(lb, h).wait_send()

            @pl.when(lb != l)
            def _():
                for h in halves:
                    z_copy(0, lb, h).wait_send()

            return carry

        lax.fori_loop(0, L, moment_sent, 0)
        for k in range(1, nf):
            for which in (0, 1, 2):
                f_copy(it, k, which).wait_send()
        return carry

    lax.fori_loop(0, ITERS, iteration, 0)


def solution(mesh):
    nf, ns = mesh.shape["feat"], mesh.shape["samp"]
    L = ns // 4

    def local(samples, factor):
        S, W = samples.shape
        B, R = factor.shape
        inv_root = 1.0 / float(S * ns) ** 0.5
        DMA = pltpu.SemaphoreType.DMA
        V = pltpu.VMEM
        peers = max(nf - 1, 1)
        scratch = [
            V((S, W), bf16),
            V((2 * L, 2 * B, R), bf16),
            V((S + R, R), f32),
            V((S + R, R), f32),
            V((S, R), bf16),
            V((S, R), bf16),
            V((ITERS, peers, S + R, R), f32),
            V((ITERS, peers, S, R), bf16),
            V((ITERS, peers, R, R), f32),
            V((2 * L, B, R), f32),
            V((2 * L, B, R), bf16),
            V((L, B, R), bf16),
            V((L, B, R), bf16),
            V((2 * L, B, R), bf16),
            V((L, B, R), bf16),
            V((2, L, B, R), bf16),
            V((B, R), f32),
            DMA,
            DMA((2 * L, 2, 2)),
            DMA((2, L, 2)),
            DMA((L, 2)),
            DMA((2 * L, 2)),
            DMA((peers, 3)),
            DMA((ITERS, peers, 3)),
            DMA((2 * L,)),
            DMA((2 * L,)),
            DMA((L, 2)),
            DMA((L, 2)),
            DMA((L, 2)),
            DMA((2, L, 2)),
        ]
        flops = ITERS * 4 * S * W * R
        previous, scaled = pl.pallas_call(
            functools.partial(kernel, L, nf, S, B, inv_root),
            out_shape=(
                jax.ShapeDtypeStruct((B, R), f32),
                jax.ShapeDtypeStruct((B, R), f32),
            ),
            in_specs=[
                pl.BlockSpec(memory_space=pl.ANY),
                pl.BlockSpec(memory_space=pltpu.VMEM),
            ],
            out_specs=(
                pl.BlockSpec(memory_space=pltpu.VMEM),
                pl.BlockSpec(memory_space=pltpu.VMEM),
            ),
            scratch_shapes=scratch,
            compiler_params=pltpu.CompilerParams(
                collective_id=0, has_side_effects=True, vmem_limit_bytes=56 * 2**20
            ),
            cost_estimate=pl.CostEstimate(
                flops=flops, bytes_accessed=2 * S * W, transcendentals=0
            ),
        )(samples, factor)
        gradient = scaled * inv_root
        return (previous + step_size * gradient, gradient)

    in_specs = (P("samp", "feat"), P(("feat", "samp"), None))
    out_specs = (P(("feat", "samp"), None), P(("feat", "samp"), None))
    return jax.shard_map(local, mesh=mesh, in_specs=in_specs, out_specs=out_specs, check_vma=False)
```
